32 devices in a mesh: row: 4 (over z), col: 8 (over y, x, core).
Axes of the slice: x: 2, y: 2, z: 4, core: 2. Of those that a mesh axis runs over, the one named last changes fastest.
Arguments:
- tokens_in: bfloat16 [192, 12288], P('col', 'row'), may hold values from -6 to 6
- w_in: bfloat16 [12288, 49152], P('row', 'col'), may hold values from -0.0546875 to 0.0546875
- b_in: float32 [49152], P('col'), may hold values from -3 to 3
- w_out: bfloat16 [49152, 12288], P('col', 'row'), may hold values from -0.02734375 to 0.02734375
- b_out: float32 [12288], P('row'), may hold values from -3 to 3
Outputs:
- tokens_out: bfloat16 [192, 12288], P('col', 'row')
The draws below stay inside these ranges and needn't reach their ends.
All inputs are finite; a program needn't handle non-finite values.
Results may differ from the reference program's by a relative error of at most 0.028.
Values may be sent and summed in bfloat16 or wider, within the bound.
No kernel may reach another device: no remote copies, remote signals or barrier semaphores. Data moves between devices by JAX's collectives and lax.ppermute only.
A program may use at most 128 MiB of HBM per device.

```python
import jax
import jax.numpy as jnp
from jax import lax

D = 12288
FF = 49152
TOKENS = 192
N_ROW = 4
N_COL = 8


def block_scale(key, shape, shards, smallest, high):
    def one(dim, parts):
        steps = jax.random.uniform(jax.random.fold_in(jax.random.fold_in(key, 6), dim), (parts,), jnp.float32, smallest / len(shards), high / len(shards))
        return jnp.repeat(jnp.exp(steps), shape[dim] // parts).reshape((-1,) + (1,) * (len(shape) - dim - 1))

    gain = one(*shards[0])
    for cut in shards[1:]:
        gain = gain * one(*cut)
    return gain


def gaussian(key, dims, width, limit, shards=(), held_as=jnp.bfloat16):
    values = jax.random.normal(key, dims, jnp.float32) * width
    if len(shards) > 0:
        values = block_scale(key, dims, shards, -0.22, 0.18) * values
    return jnp.clip(values, min=-limit, max=limit).astype(held_as)


def setup_inputs(seed: int = 0) -> dict:
    key_list = jax.random.split(jax.random.key(seed), 6)
    tokens_in = gaussian(key_list[0], (TOKENS, D), 1.0, 6.0, ((0, 8), (1, 4)))
    w_in = gaussian(key_list[1], (D, FF), D ** -0.5, 0.0546875, ((0, 4), (1, 8)))
    b_in = gaussian(key_list[2], (FF,), 0.5, 3.0, ((0, 8),), jnp.float32)
    w_out = gaussian(key_list[3], (FF, D), FF ** -0.5, 0.02734375, ((0, 8), (1, 4)))
    b_out = gaussian(key_list[4], (D,), 0.5, 3.0, ((0, 4),), jnp.float32)
    return {"tokens_in": tokens_in, "w_in": w_in, "b_in": b_in, "w_out": w_out, "b_out": b_out}


def block_sum(left, right, total):
    def step(acc, pair):
        part = jnp.dot(pair[0], pair[1], preferred_element_type=jnp.float32).astype(jnp.bfloat16)
        part = lax.optimization_barrier(part)
        return acc + part.astype(jnp.float32), None
    result, _ = lax.scan(step, total, (left, right))
    return result


def reference(tokens_in, w_in, b_in, w_out, b_out):
    x_blocks = tokens_in.reshape(TOKENS, N_ROW, D // N_ROW).transpose(1, 0, 2)
    w_blocks = w_in.reshape(N_ROW, D // N_ROW, FF)
    pre = block_sum(x_blocks, w_blocks, jnp.zeros((TOKENS, FF), jnp.float32)) + b_in.astype(jnp.float32)
    hidden = jax.nn.gelu(pre, approximate=True).astype(jnp.bfloat16)
    h_blocks = hidden.reshape(TOKENS, N_COL, FF // N_COL).transpose(1, 0, 2)
    v_blocks = w_out.reshape(N_COL, FF // N_COL, D)
    total = block_sum(h_blocks, v_blocks, jnp.zeros((TOKENS, D), jnp.float32)) + b_out.astype(jnp.float32)
    return total.astype(jnp.bfloat16)
```

```python
import functools

import jax
import jax.numpy as jnp
from jax import lax
from jax.experimental import pallas as pl
from jax.experimental.pallas import tpu as pltpu
from jax.sharding import PartitionSpec as P

F32 = jnp.float32
BF16 = jnp.bfloat16


def chunks(width, shares, unit):
    units = width // unit
    ends = [round(units * sum(shares[:i]) / sum(shares)) for i in range(len(shares) + 1)]
    cuts = [unit * e for e in ends[:-1]] + [width]
    return [(lo, hi) for lo, hi in zip(cuts, cuts[1:]) if hi > lo]


TURNS = (
    (0, 0), (1, 0), (2, 0), (0, 1), (3, 0), (1, 1), (0, 2), (4, 0),
    (2, 1), (1, 2), (5, 0), (3, 1), (2, 2), (4, 1), (0, 3), (3, 2),
    (5, 1), (4, 2), (1, 3), (2, 3), (5, 2), (3, 3), (4, 3), (5, 3),
)


def plan(count, low):
    last = 2 * low + 1
    turns = [(2 * t + 2 * step, -t, t, step) for t in range(count) for step in range(last + 1)]
    return [(t, step) for _, _, t, step in sorted(turns)]


def nothing(*refs):
    pass


def after(x, *others):
    others = [o for o in others if o is not None]
    return pl.pallas_call(
        nothing,
        in_specs=[pl.BlockSpec(memory_space=pl.ANY)] * (1 + len(others)),
        out_specs=pl.BlockSpec(memory_space=pl.ANY),
        out_shape=jax.ShapeDtypeStruct(x.shape, x.dtype),
        input_output_aliases={0: 0},
        cost_estimate=pl.CostEstimate(flops=0, bytes_accessed=0, transcendentals=0),
        compiler_params=pltpu.CompilerParams(vmem_limit_bytes=1 << 20),
    )(x, *others)


def fetch_kernel(lo, hi, dim, w_ref, *refs):
    o_ref, sem = refs[-2:]
    depth = o_ref.shape[0] // sem.shape[0]
    copies = []
    for i in range(sem.shape[0]):
        rows = pl.ds(i * depth, depth)
        source = w_ref.at[rows, pl.ds(lo, hi - lo)] if dim else w_ref.at[pl.ds(lo + i * depth, depth)]
        copies.append(pltpu.make_async_copy(source, o_ref.at[rows], sem.at[i]))
        copies[-1].start()
    for copy in copies:
        copy.wait()


def fetch(w, lo, hi, *others, dim=1):
    shape = (w.shape[0], hi - lo) if dim else (hi - lo, w.shape[1])
    return pl.pallas_call(
        functools.partial(fetch_kernel, lo, hi, dim),
        in_specs=[pl.BlockSpec(memory_space=pltpu.HBM)]
        + [pl.BlockSpec(memory_space=pl.ANY)] * len(others),
        out_specs=pl.BlockSpec(memory_space=pl.ANY),
        out_shape=pltpu.VMEM(shape, w.dtype),
        scratch_shapes=[pltpu.SemaphoreType.DMA((8,))],
        cost_estimate=pl.CostEstimate(
            flops=0, bytes_accessed=4 * shape[0] * shape[1], transcendentals=0
        ),
        compiler_params=pltpu.CompilerParams(vmem_limit_bytes=1 << 20),
    )(pltpu.with_memory_space_constraint(w, pltpu.HBM), *others)


def piece(w, index, x):
    source, x = lax.optimization_barrier((w, x))
    return lax.optimization_barrier((source[index], x))


def swap(x, axis, n, mask):
    return lax.ppermute(x, axis, [(i, i ^ mask) for i in range(n)])


def gather_tokens(x, n, w, bounds):
    order = [0] + list(range(2, n, 2))
    came = [swap(x, "col", n, mask) for mask in order[:0:-1]][::-1]
    columns = []
    for lo, hi in bounds:
        columns.append(fetch(w, lo, hi, *columns[-1:]))
    if came:
        came[-1] = after(came[-1], columns[-1])
    held = jnp.concatenate([x] + came, axis=0)
    return jnp.concatenate([held, swap(held, "col", n, 1)], axis=0), columns


def scatter_sums(total, n, bias):
    half = total.shape[0] // 2
    near = total[:half].astype(F32) + swap(total[half:], "col", n, 1).astype(F32)
    rows = total.shape[0] // n
    own = near[:rows]
    for j in range(1, n // 2):
        own = own + swap(near[j * rows:(j + 1) * rows].astype(BF16), "col", n, 2 * j).astype(F32)
    return (own + bias).astype(BF16)


def add(a, b):
    return (a.astype(F32) + b.astype(F32)).astype(BF16)


def body(n_row, n_col, tokens_in, w_in, b_in, w_out, b_out):
    bounds = chunks(w_in.shape[1], (1, 1, 1, 1, 1, 1), 256)
    me = lax.axis_index("row")
    low, high = n_row // 2 - 1, n_row // 2
    ends = [((me == s) | (me == n_row - 1 - s)).reshape(1, 1) for s in range(low)]
    tokens_in, b_in, *ends = lax.optimization_barrier((tokens_in, b_in, *ends))
    x, columns = gather_tokens(tokens_in, n_col, w_in, bounds[:2])
    inward = [[(s, s + 1), (n_row - 1 - s, n_row - 2 - s)] for s in range(low)]
    middle = [(low, high), (high, low)]
    held, rows = {}, {}
    total, last = None, None
    turns = TURNS if (len(bounds), low) == (6, 1) else plan(len(bounds), low)
    for t, step in turns:
        lo, hi = bounds[t]
        if step == 0:
            x = after(x, last)
            held[t] = jnp.dot(x, columns[t], preferred_element_type=F32).astype(BF16)
        elif step <= low:
            came = after(lax.ppermute(held[t], "row", inward[step - 1]), last)
            held[t] = add(held[t], came)
        elif step == high:
            came = after(lax.ppermute(held[t], "row", middle), last)
            pre = held[t].astype(F32) + came.astype(F32) + b_in[lo:hi]
            held[t] = jax.nn.gelu(pre, approximate=True).astype(BF16)
        else:
            s = 2 * low + 1 - step
            came = after(lax.ppermute(held[t], "row", [(b, a) for a, b in inward[s]]), last)
            held[t] = jnp.where(ends[s], came, held[t])
        last = held[t]
        if step == 2 * low + 1:
            out = jnp.dot(held[t], rows[t], preferred_element_type=F32)
            last = total = out if total is None else total + out
            if t + 1 < len(bounds):
                rows[t + 1], last = piece(w_out, slice(*bounds[t + 1]), last)
        elif step == high and t == 0:
            rows[0], last = piece(w_out, slice(*bounds[0]), last)
        elif step == 0 and t:
            while len(columns) < min(t + 3, len(bounds)):
                w, last = piece(w_in, (slice(None), slice(*bounds[len(columns)])), last)
                columns.append(w)
    return scatter_sums(total.astype(BF16), n_col, b_out)


def solution(mesh):
    placed = (P("col", "row"), P("row", "col"), P("col"), P("col", "row"), P("row"))
    return jax.shard_map(
        functools.partial(body, mesh.shape["row"], mesh.shape["col"]),
        mesh=mesh,
        in_specs=placed,
        out_specs=P("col", "row"),
        check_vma=False,
    )
```

```python
import functools

import jax
import jax.numpy as jnp
from jax import lax
from jax.experimental import pallas as pl
from jax.experimental.pallas import tpu as pltpu
from jax.sharding import PartitionSpec as P

F32 = jnp.float32
BF16 = jnp.bfloat16


def chunks(width, shares, unit):
    units = width // unit
    ends = [round(units * sum(shares[:i]) / sum(shares)) for i in range(len(shares) + 1)]
    cuts = [unit * e for e in ends[:-1]] + [width]
    return [(lo, hi) for lo, hi in zip(cuts, cuts[1:]) if hi > lo]


TURNS = (
    (0, 0), (1, 0), (2, 0), (3, 0), (0, 1), (4, 0), (1, 1), (0, 2),
    (2, 1), (1, 2), (5, 0), (3, 1), (0, 3), (2, 2), (4, 1), (1, 3),
    (3, 2), (5, 1), (2, 3), (4, 2), (3, 3), (5, 2), (4, 3), (5, 3),
)


def plan(count, low):
    last = 2 * low + 1
    turns = [(2 * t + 2 * step, -t, t, step) for t in range(count) for step in range(last + 1)]
    return [(t, step) for _, _, t, step in sorted(turns)]


def nothing(*refs):
    pass


def after(x, *others):
    others = [o for o in others if o is not None]
    return pl.pallas_call(
        nothing,
        in_specs=[pl.BlockSpec(memory_space=pl.ANY)] * (1 + len(others)),
        out_specs=pl.BlockSpec(memory_space=pl.ANY),
        out_shape=jax.ShapeDtypeStruct(x.shape, x.dtype),
        input_output_aliases={0: 0},
        cost_estimate=pl.CostEstimate(flops=0, bytes_accessed=0, transcendentals=0),
        compiler_params=pltpu.CompilerParams(vmem_limit_bytes=1 << 20),
    )(x, *others)


def fetch_kernel(lo, hi, dim, w_ref, *refs):
    o_ref, sem = refs[-2:]
    depth = o_ref.shape[0] // sem.shape[0]
    copies = []
    for i in range(sem.shape[0]):
        rows = pl.ds(i * depth, depth)
        source = w_ref.at[rows, pl.ds(lo, hi - lo)] if dim else w_ref.at[pl.ds(lo + i * depth, depth)]
        copies.append(pltpu.make_async_copy(source, o_ref.at[rows], sem.at[i]))
        copies[-1].start()
    for copy in copies:
        copy.wait()


def fetch(w, lo, hi, *others, dim=1):
    shape = (w.shape[0], hi - lo) if dim else (hi - lo, w.shape[1])
    return pl.pallas_call(
        functools.partial(fetch_kernel, lo, hi, dim),
        in_specs=[pl.BlockSpec(memory_space=pltpu.HBM)]
        + [pl.BlockSpec(memory_space=pl.ANY)] * len(others),
        out_specs=pl.BlockSpec(memory_space=pl.ANY),
        out_shape=pltpu.VMEM(shape, w.dtype),
        scratch_shapes=[pltpu.SemaphoreType.DMA((8,))],
        cost_estimate=pl.CostEstimate(
            flops=0, bytes_accessed=4 * shape[0] * shape[1], transcendentals=0
        ),
        compiler_params=pltpu.CompilerParams(vmem_limit_bytes=1 << 20),
    )(pltpu.with_memory_space_constraint(w, pltpu.HBM), *others)


def piece(w, index, x):
    source, x = lax.optimization_barrier((w, x))
    return lax.optimization_barrier((source[index], x))


def swap(x, axis, n, mask):
    return lax.ppermute(x, axis, [(i, i ^ mask) for i in range(n)])


def gather_tokens(x, n, w, bounds):
    came = [swap(x, "col", n, mask) for mask in range(2, n, 2)]
    columns = []
    for lo, hi in bounds:
        columns.append(fetch(w, lo, hi, *columns[-1:]))
    blocks = [x] + [after(block, columns[-1]) for block in came]
    blocks += [swap(block, "col", n, 1) for block in blocks]
    return jnp.concatenate(blocks, axis=0), columns


def scatter_sums(total, n, bias):
    half = total.shape[0] // 2
    near = total[:half].astype(F32) + swap(total[half:], "col", n, 1).astype(F32)
    rows = total.shape[0] // n
    own = near[:rows]
    for j in range(1, n // 2):
        own = own + swap(near[j * rows:(j + 1) * rows].astype(BF16), "col", n, 2 * j).astype(F32)
    return (own + bias).astype(BF16)


def add(a, b):
    return (a.astype(F32) + b.astype(F32)).astype(BF16)


def body(n_row, n_col, tokens_in, w_in, b_in, w_out, b_out):
    bounds = chunks(w_in.shape[1], (1, 1, 1, 1, 1, 1), 256)
    me = lax.axis_index("row")
    low, high = n_row // 2 - 1, n_row // 2
    ends = [((me == s) | (me == n_row - 1 - s)).reshape(1, 1) for s in range(low)]
    tokens_in, b_in, *ends = lax.optimization_barrier((tokens_in, b_in, *ends))
    x, columns = gather_tokens(tokens_in, n_col, w_in, bounds[:2])
    inward = [[(s, s + 1), (n_row - 1 - s, n_row - 2 - s)] for s in range(low)]
    middle = [(low, high), (high, low)]
    held, rows = {}, {}
    total, last = None, None
    turns = TURNS if (len(bounds), low) == (6, 1) else plan(len(bounds), low)
    for t, step in turns:
        lo, hi = bounds[t]
        if step == 0:
            x = after(x, last)
            held[t] = jnp.dot(x, columns[t], preferred_element_type=F32).astype(BF16)
        elif step <= low:
            came = after(lax.ppermute(held[t], "row", inward[step - 1]), last)
            held[t] = add(held[t], came)
        elif step == high:
            came = after(lax.ppermute(held[t], "row", middle), last)
            pre = held[t].astype(F32) + came.astype(F32) + b_in[lo:hi]
            held[t] = jax.nn.gelu(pre, approximate=True).astype(BF16)
        else:
            s = 2 * low + 1 - step
            came = after(lax.ppermute(held[t], "row", [(b, a) for a, b in inward[s]]), last)
            held[t] = jnp.where(ends[s], came, held[t])
        last = held[t]
        if step == 2 * low + 1:
            out = jnp.dot(held[t], rows[t], preferred_element_type=F32)
            last = total = out if total is None else total + out
            if t + 1 < len(bounds):
                rows[t + 1], last = piece(w_out, slice(*bounds[t + 1]), last)
        elif step == high and t == 0:
            rows[0], last = piece(w_out, slice(*bounds[0]), last)
        elif step == 0 and t:
            while len(columns) < min(t + 3, len(bounds)):
                w, last = piece(w_in, (slice(None), slice(*bounds[len(columns)])), last)
                columns.append(w)
    return scatter_sums(total.astype(BF16), n_col, b_out)


def solution(mesh):
    placed = (P("col", "row"), P("row", "col"), P("col"), P("col", "row"), P("row"))
    return jax.shard_map(
        functools.partial(body, mesh.shape["row"], mesh.shape["col"]),
        mesh=mesh,
        in_specs=placed,
        out_specs=P("col", "row"),
        check_vma=False,
    )
```

```python
import functools

import jax
import jax.numpy as jnp
from jax import lax
from jax.experimental import pallas as pl
from jax.experimental.pallas import tpu as pltpu
from jax.sharding import PartitionSpec as P

F32 = jnp.float32
BF16 = jnp.bfloat16


def chunks(width, shares, unit):
    units = width // unit
    ends = [round(units * sum(shares[:i]) / sum(shares)) for i in range(len(shares) + 1)]
    cuts = [unit * e for e in ends[:-1]] + [width]
    return [(lo, hi) for lo, hi in zip(cuts, cuts[1:]) if hi > lo]


TURNS = (
    (0, 0), (1, 0), (2, 0), (3, 0), (0, 1), (4, 0), (1, 1), (0, 2),
    (2, 1), (1, 2), (5, 0), (3, 1), (0, 3), (2, 2), (4, 1), (1, 3),
    (3, 2), (5, 1), (2, 3), (4, 2), (3, 3), (5, 2), (4, 3), (5, 3),
)


def plan(count, low):
    last = 2 * low + 1
    turns = [(2 * t + 2 * step, -t, t, step) for t in range(count) for step in range(last + 1)]
    return [(t, step) for _, _, t, step in sorted(turns)]


def nothing(*refs):
    pass


def after(x, *others):
    others = [o for o in others if o is not None]
    return pl.pallas_call(
        nothing,
        in_specs=[pl.BlockSpec(memory_space=pl.ANY)] * (1 + len(others)),
        out_specs=pl.BlockSpec(memory_space=pl.ANY),
        out_shape=jax.ShapeDtypeStruct(x.shape, x.dtype),
        input_output_aliases={0: 0},
        cost_estimate=pl.CostEstimate(flops=0, bytes_accessed=0, transcendentals=0),
        compiler_params=pltpu.CompilerParams(vmem_limit_bytes=1 << 20),
    )(x, *others)


def fetch_kernel(lo, hi, dim, w_ref, *refs):
    o_ref, sem = refs[-2:]
    depth = o_ref.shape[0] // sem.shape[0]
    copies = []
    for i in range(sem.shape[0]):
        rows = pl.ds(i * depth, depth)
        source = w_ref.at[rows, pl.ds(lo, hi - lo)] if dim else w_ref.at[pl.ds(lo + i * depth, depth)]
        copies.append(pltpu.make_async_copy(source, o_ref.at[rows], sem.at[i]))
        copies[-1].start()
    for copy in copies:
        copy.wait()


def fetch(w, lo, hi, *others, dim=1):
    shape = (w.shape[0], hi - lo) if dim else (hi - lo, w.shape[1])
    return pl.pallas_call(
        functools.partial(fetch_kernel, lo, hi, dim),
        in_specs=[pl.BlockSpec(memory_space=pltpu.HBM)]
        + [pl.BlockSpec(memory_space=pl.ANY)] * len(others),
        out_specs=pl.BlockSpec(memory_space=pl.ANY),
        out_shape=pltpu.VMEM(shape, w.dtype),
        scratch_shapes=[pltpu.SemaphoreType.DMA((8,))],
        cost_estimate=pl.CostEstimate(
            flops=0, bytes_accessed=4 * shape[0] * shape[1], transcendentals=0
        ),
        compiler_params=pltpu.CompilerParams(vmem_limit_bytes=1 << 20),
    )(pltpu.with_memory_space_constraint(w, pltpu.HBM), *others)


def piece(w, index, x):
    source, x = lax.optimization_barrier((w, x))
    return lax.optimization_barrier((source[index], x))


def swap(x, axis, n, mask):
    return lax.ppermute(x, axis, [(i, i ^ mask) for i in range(n)])


def gather_tokens(x, n, w, bounds):
    came = [swap(x, "col", n, mask) for mask in range(2, n, 2)]
    columns = []
    for lo, hi in bounds:
        columns.append(fetch(w, lo, hi, *columns[-1:]))
    blocks = [x] + [after(block, columns[-1]) for block in came]
    blocks += [swap(block, "col", n, 1) for block in blocks]
    return jnp.concatenate(blocks, axis=0), columns


def scatter_sums(total, n, bias):
    half = total.shape[0] // 2
    near = total[:half].astype(F32) + swap(total[half:], "col", n, 1).astype(F32)
    rows = total.shape[0] // n
    own = near[:rows]
    for j in range(1, n // 2):
        own = own + swap(near[j * rows:(j + 1) * rows].astype(BF16), "col", n, 2 * j).astype(F32)
    return (own + bias).astype(BF16)


def add(a, b):
    return (a.astype(F32) + b.astype(F32)).astype(BF16)


def body(n_row, n_col, tokens_in, w_in, b_in, w_out, b_out):
    bounds = chunks(w_in.shape[1], (8, 8, 8, 9, 9, 6), 128)
    me = lax.axis_index("row")
    low, high = n_row // 2 - 1, n_row // 2
    ends = [((me == s) | (me == n_row - 1 - s)).reshape(1, 1) for s in range(low)]
    tokens_in, b_in, *ends = lax.optimization_barrier((tokens_in, b_in, *ends))
    x, columns = gather_tokens(tokens_in, n_col, w_in, bounds[:2])
    inward = [[(s, s + 1), (n_row - 1 - s, n_row - 2 - s)] for s in range(low)]
    middle = [(low, high), (high, low)]
    held, rows = {}, {}
    total, last = None, None
    turns = TURNS if (len(bounds), low) == (6, 1) else plan(len(bounds), low)
    for t, step in turns:
        lo, hi = bounds[t]
        if step == 0:
            x = after(x, last)
            held[t] = jnp.dot(x, columns[t], preferred_element_type=F32).astype(BF16)
        elif step <= low:
            came = after(lax.ppermute(held[t], "row", inward[step - 1]), last)
            held[t] = add(held[t], came)
        elif step == high:
            came = after(lax.ppermute(held[t], "row", middle), last)
            pre = held[t].astype(F32) + came.astype(F32) + b_in[lo:hi]
            held[t] = jax.nn.gelu(pre, approximate=True).astype(BF16)
        else:
            s = 2 * low + 1 - step
            came = after(lax.ppermute(held[t], "row", [(b, a) for a, b in inward[s]]), last)
            held[t] = jnp.where(ends[s], came, held[t])
        last = held[t]
        if step == 0 and t == 0:
            b_in = after(b_in, last)
        if step == 2 * low + 1:
            out = jnp.dot(held[t], rows[t], preferred_element_type=F32)
            last = total = out if total is None else total + out
            if t + 1 < len(bounds):
                rows[t + 1], last = piece(w_out, slice(*bounds[t + 1]), last)
        elif step == high and t == 0:
            rows[0], last = piece(w_out, slice(*bounds[0]), last)
        elif step == 0 and t:
            while len(columns) < min(t + 3, len(bounds)):
                w, last = piece(w_in, (slice(None), slice(*bounds[len(columns)])), last)
                columns.append(w)
    return scatter_sums(total.astype(BF16), n_col, b_out)


def solution(mesh):
    placed = (P("col", "row"), P("row", "col"), P("col"), P("col", "row"), P("row"))
    return jax.shard_map(
        functools.partial(body, mesh.shape["row"], mesh.shape["col"]),
        mesh=mesh,
        in_specs=placed,
        out_specs=P("col", "row"),
        check_vma=False,
    )
```

```python
import functools

import jax
import jax.numpy as jnp
from jax import lax
from jax.experimental import pallas as pl
from jax.experimental.pallas import tpu as pltpu
from jax.sharding import PartitionSpec as P

F32 = jnp.float32
BF16 = jnp.bfloat16


def chunks(width, shares, unit):
    units = width // unit
    ends = [round(units * sum(shares[:i]) / sum(shares)) for i in range(len(shares) + 1)]
    cuts = [unit * e for e in ends[:-1]] + [width]
    return [(lo, hi) for lo, hi in zip(cuts, cuts[1:]) if hi > lo]


TURNS = (
    (0, 0), (1, 0), (2, 0), (0, 1), (3, 0), (1, 1), (0, 2), (4, 0),
    (2, 1), (1, 2), (5, 0), (3, 1), (2, 2), (4, 1), (0, 3), (3, 2),
    (5, 1), (4, 2), (1, 3), (2, 3), (5, 2), (3, 3), (4, 3), (5, 3),
)


def plan(count, low):
    last = 2 * low + 1
    turns = [(2 * t + 2 * step, -t, t, step) for t in range(count) for step in range(last + 1)]
    return [(t, step) for _, _, t, step in sorted(turns)]


def nothing(*refs):
    pass


def after(x, *others):
    others = [o for o in others if o is not None]
    return pl.pallas_call(
        nothing,
        in_specs=[pl.BlockSpec(memory_space=pl.ANY)] * (1 + len(others)),
        out_specs=pl.BlockSpec(memory_space=pl.ANY),
        out_shape=jax.ShapeDtypeStruct(x.shape, x.dtype),
        input_output_aliases={0: 0},
        cost_estimate=pl.CostEstimate(flops=0, bytes_accessed=0, transcendentals=0),
        compiler_params=pltpu.CompilerParams(vmem_limit_bytes=1 << 20),
    )(x, *others)


def fetch_kernel(lo, hi, dim, w_ref, *refs):
    o_ref, sem = refs[-2:]
    depth = o_ref.shape[0] // sem.shape[0]
    copies = []
    for i in range(sem.shape[0]):
        rows = pl.ds(i * depth, depth)
        source = w_ref.at[rows, pl.ds(lo, hi - lo)] if dim else w_ref.at[pl.ds(lo + i * depth, depth)]
        copies.append(pltpu.make_async_copy(source, o_ref.at[rows], sem.at[i]))
        copies[-1].start()
    for copy in copies:
        copy.wait()


def fetch(w, lo, hi, *others, dim=1):
    shape = (w.shape[0], hi - lo) if dim else (hi - lo, w.shape[1])
    return pl.pallas_call(
        functools.partial(fetch_kernel, lo, hi, dim),
        in_specs=[pl.BlockSpec(memory_space=pltpu.HBM)]
        + [pl.BlockSpec(memory_space=pl.ANY)] * len(others),
        out_specs=pl.BlockSpec(memory_space=pl.ANY),
        out_shape=pltpu.VMEM(shape, w.dtype),
        scratch_shapes=[pltpu.SemaphoreType.DMA((8,))],
        cost_estimate=pl.CostEstimate(
            flops=0, bytes_accessed=4 * shape[0] * shape[1], transcendentals=0
        ),
        compiler_params=pltpu.CompilerParams(vmem_limit_bytes=1 << 20),
    )(pltpu.with_memory_space_constraint(w, pltpu.HBM), *others)


def piece(w, index, x):
    source, x = lax.optimization_barrier((w, x))
    return lax.optimization_barrier((source[index], x))


def swap(x, axis, n, mask):
    return lax.ppermute(x, axis, [(i, i ^ mask) for i in range(n)])


def gather_tokens(x, n, w, bounds):
    order = [0] + list(range(2, n, 2))
    came = [swap(x, "col", n, mask) for mask in order[:0:-1]][::-1]
    columns = []
    for lo, hi in bounds:
        columns.append(fetch(w, lo, hi, *columns[-1:]))
    if came:
        came[-1] = after(came[-1], columns[-1])
    held = jnp.concatenate([x] + came, axis=0)
    return jnp.concatenate([held, swap(held, "col", n, 1)], axis=0), columns


def scatter_sums(total, n, bias):
    theirs, mine = total
    near = mine.astype(F32) + swap(theirs, "col", n, 1).astype(F32)
    rows = 2 * mine.shape[0] // n
    own = near[:rows]
    for j in range(1, n // 2):
        own = own + swap(near[j * rows:(j + 1) * rows].astype(BF16), "col", n, 2 * j).astype(F32)
    return (own + bias).astype(BF16)


def add(a, b):
    return (a.astype(F32) + b.astype(F32)).astype(BF16)


def body(n_row, n_col, tokens_in, w_in, b_in, w_out, b_out):
    bounds = chunks(w_in.shape[1], (1, 1, 1, 1, 1, 1), 256)
    me = lax.axis_index("row")
    low, high = n_row // 2 - 1, n_row // 2
    ends = [((me == s) | (me == n_row - 1 - s)).reshape(1, 1) for s in range(low)]
    tokens_in, b_in, *ends = lax.optimization_barrier((tokens_in, b_in, *ends))
    x, columns = gather_tokens(tokens_in, n_col, w_in, bounds[:2])
    inward = [[(s, s + 1), (n_row - 1 - s, n_row - 2 - s)] for s in range(low)]
    middle = [(low, high), (high, low)]
    held, rows = {}, {}
    total, last = None, None
    turns = TURNS if (len(bounds), low) == (6, 1) else plan(len(bounds), low)
    for t, step in turns:
        lo, hi = bounds[t]
        if step == 0:
            x = after(x, last)
            held[t] = jnp.dot(x, columns[t], preferred_element_type=F32).astype(BF16)
        elif step <= low:
            came = after(lax.ppermute(held[t], "row", inward[step - 1]), last)
            held[t] = add(held[t], came)
        elif step == high:
            came = after(lax.ppermute(held[t], "row", middle), last)
            pre = held[t].astype(F32) + came.astype(F32) + b_in[lo:hi]
            held[t] = jax.nn.gelu(pre, approximate=True).astype(BF16)
        else:
            s = 2 * low + 1 - step
            came = after(lax.ppermute(held[t], "row", [(b, a) for a, b in inward[s]]), last)
            held[t] = jnp.where(ends[s], came, held[t])
        last = held[t]
        if step == 2 * low + 1 and t + 1 == len(bounds):
            half, sums = x.shape[0] // 2, []
            for part in (slice(half, None), slice(0, half)):
                chunk = after(held[t][part], *sums)
                out = jnp.dot(chunk, rows[t], preferred_element_type=F32)
                sums.append((total[part] + out).astype(BF16))
        elif step == 2 * low + 1:
            out = jnp.dot(held[t], rows[t], preferred_element_type=F32)
            last = total = out if total is None else total + out
            if t + 1 < len(bounds):
                rows[t + 1], last = piece(w_out, slice(*bounds[t + 1]), last)
        elif step == high and t == 0:
            rows[0], last = piece(w_out, slice(*bounds[0]), last)
        elif step == 0 and t:
            while len(columns) < min(t + 3, len(bounds)):
                w, last = piece(w_in, (slice(None), slice(*bounds[len(columns)])), last)
                columns.append(w)
    return scatter_sums(sums, n_col, b_out)


def solution(mesh):
    placed = (P("col", "row"), P("row", "col"), P("col"), P("col", "row"), P("row"))
    return jax.shard_map(
        functools.partial(body, mesh.shape["row"], mesh.shape["col"]),
        mesh=mesh,
        in_specs=placed,
        out_specs=P("col", "row"),
        check_vma=False,
    )
```
